32 devices in a mesh: mem: 2 (over core), lat: 16 (over z, y, x).
Axes of the slice: x: 2, y: 2, z: 4, core: 2. Of those that a mesh axis runs over, the one named last changes fastest.
Arguments:
- members: bfloat16 [8, 4, 16, 128, 1024], P('mem', None, None, 'lat'), may hold values from -6 to 6
- increment: float32 [4, 16, 128, 1024], P(None, 'mem', 'lat'), may hold values from -6 to 6
- vertical: float32 [16, 16], replicated, may hold values from -1.5 to 1.5
- lat_taps: float32 [9], replicated, may hold values from 0.2 to 0.6
- lon_taps: float32 [9], replicated, may hold values from 0.2 to 0.6
Outputs:
- product: float32 [4, 16, 128, 1024], P(None, 'mem', 'lat')
The draws below stay inside these ranges and needn't reach their ends.
All inputs are finite; a program needn't handle non-finite values.
Results may differ from the reference program's by a relative error of at most 0.0003.
Values sent between devices are 32-bit elements; how exact they have to be, the bound alone decides.
A program may use at most 64 MiB of HBM per device.

```python
import jax
import jax.numpy as jnp
from jax import lax

VARS = 4
LEV = 16
TAPS = 9
LON = 1024
MEMBERS = 8
LAT = 128


def shard_levels(rng, extent, pieces, least, high):
    factor_of, own = 1.0, jax.random.fold_in(rng, 6)
    for position, shards_of in pieces:
        heights = jnp.exp(jax.random.uniform(jax.random.fold_in(own, position), (shards_of,), jnp.float32, least / len(pieces), high / len(pieces)))
        factor_of = factor_of * jnp.repeat(heights, extent[position] // shards_of).reshape([-1 if axis == position else 1 for axis in range(len(extent))])
    return factor_of


def gaussian(stream_key, extent, width, reach, pieces=(), held_as=jnp.bfloat16):
    entries = jax.random.normal(stream_key, extent, jnp.float32) * width
    if len(pieces) > 0:
        entries = shard_levels(stream_key, extent, pieces, -0.22, 0.18) * entries
    return jnp.clip(entries, min=-reach, max=reach).astype(held_as)


def setup_inputs(seed: int = 0) -> dict:
    arg_keys = jax.random.split(jax.random.key(seed), 6)
    members = gaussian(arg_keys[0], (MEMBERS, VARS, LEV, LAT, LON), 1.0, 6.0, ((0, 2), (3, 16)))
    increment = gaussian(arg_keys[1], (VARS, LEV, LAT, LON), 1.0, 6.0, ((1, 2), (2, 16)), jnp.float32)
    vertical = gaussian(arg_keys[2], (LEV, LEV), LEV ** -0.5, 1.5, (), jnp.float32)
    lat_taps = jnp.clip(jax.random.uniform(arg_keys[3], (TAPS,), jnp.float32, 0.2, 0.6), 0.2, 0.6)
    lon_taps = jnp.clip(jax.random.uniform(arg_keys[4], (TAPS,), jnp.float32, 0.2, 0.6), 0.2, 0.6)
    return {"members": members, "increment": increment, "vertical": vertical, "lat_taps": lat_taps, "lon_taps": lon_taps}


def lon_adjoint(source, kernel):
    summed = jnp.zeros(source.shape, jnp.float32)
    for offset in range(9):
        summed = summed + kernel[offset] * jnp.roll(source, offset - 4, axis=-1)
    return summed


def lon_forward(source, kernel):
    summed = jnp.zeros(source.shape, jnp.float32)
    for offset in range(9):
        summed = summed + kernel[offset] * jnp.roll(source, 4 - offset, axis=-1)
    return summed


def lat_adjoint(padded, kernel):
    row_count = padded.shape[-2] - 8
    summed = kernel[0] * padded[..., 8:8 + row_count, :]
    for offset in range(1, 9):
        summed = summed + kernel[offset] * padded[..., 8 - offset:8 - offset + row_count, :]
    return summed


def lat_forward(padded, kernel):
    row_count = padded.shape[-2] - 8
    summed = kernel[0] * padded[..., 0:row_count, :]
    for offset in range(1, 9):
        summed = summed + kernel[offset] * padded[..., offset:offset + row_count, :]
    return summed


def pad_rows(source):
    return jnp.pad(source, ((0, 0), (4, 4), (0, 0)))


def reference(members, increment, vertical, lat_taps, lon_taps):
    def member_step(summed, member):
        values = member.astype(jnp.float32)
        weighted = jnp.sum(values * increment, axis=0)
        weighted = lon_adjoint(weighted, lon_taps)
        weighted = jnp.einsum("kl,kij->lij", vertical, weighted, precision=lax.Precision.HIGHEST)
        adjoint_field = lat_adjoint(pad_rows(weighted), lat_taps)
        spread = lat_forward(pad_rows(adjoint_field), lat_taps)
        spread = lon_forward(spread, lon_taps)
        spread = jnp.einsum("lk,kij->lij", vertical, spread, precision=lax.Precision.HIGHEST)
        return summed + values * spread[None], None

    summed, unused = lax.scan(member_step, jnp.zeros(increment.shape, jnp.float32), members)
    return summed / (MEMBERS - 1)
```

```python
import functools

import jax
import jax.numpy as jnp
from jax import lax
from jax.experimental import pallas as pl
from jax.experimental.pallas import tpu as pltpu
from jax.sharding import PartitionSpec as P

LANES = 128
PIECE = 16
HIGHEST = lax.Precision.HIGHEST
MESH = pl.DeviceIdType.MESH


def kernel(
    n_mem, n_lat, levels, members_ref, inc_ref, vert_ref, lat_ref, lon_ref, out_ref,
    mem_v, inc_v, own, buf, acc, part, mats,
    load_sem, inc_sem, inc_send, inc_recv, xs, xr, ys, yr, zs, zr, ps, pr,
):
    count, variables, rows, lon = mem_v.shape
    slab = rows // levels
    taps = lat_ref.shape[0]
    reach = taps // 2
    chunks = lon // LANES
    items = count * chunks
    share = rows // n_mem
    me = lax.axis_index("mem")
    i = lax.axis_index("lat")
    x = lax.rem(i, 2)
    y = lax.rem(lax.div(i, 2), 2)
    x_peer = i + 1 - 2 * x
    y_peer = i + 2 - 4 * y
    corner = x == y
    z_target = i + 4 - 8 * x
    z_source = i - 4 + 8 * x
    z_out = corner & (z_target >= 0) & (z_target < n_lat)
    z_in = corner & (z_source >= 0) & (z_source < n_lat)

    def load(m):
        return pltpu.make_async_copy(members_ref.at[m], mem_v.at[m], load_sem.at[m])

    own_rows = pl.ds(pl.multiple_of(me * share, share), share)
    inc_local = pltpu.make_async_copy(inc_ref, inc_v.at[:, own_rows, :], inc_sem)
    inc_local.start()
    for m in range(count):
        load(m).start()

    barrier = pltpu.get_barrier_semaphore()
    for k in range(1, n_mem):
        pl.semaphore_signal(
            barrier, inc=1, device_id={"mem": lax.rem(me + k, n_mem)}, device_id_type=MESH
        )
    pl.semaphore_signal(barrier, inc=1, device_id={"lat": x_peer}, device_id_type=MESH)
    pl.semaphore_signal(barrier, inc=1, device_id={"lat": y_peer}, device_id_type=MESH)

    @pl.when(z_out)
    def _():
        pl.semaphore_signal(barrier, inc=1, device_id={"lat": z_target}, device_id_type=MESH)

    @pl.when(z_in)
    def _():
        pl.semaphore_signal(barrier, inc=1, device_id={"lat": z_source}, device_id_type=MESH)

    pl.semaphore_wait(barrier, n_mem + 1 + z_out.astype(jnp.int32) + z_in.astype(jnp.int32))

    def inc_copy(k):
        return pltpu.make_async_remote_copy(
            src_ref=inc_ref,
            dst_ref=inc_v.at[:, own_rows, :],
            send_sem=inc_send.at[k - 1],
            recv_sem=inc_recv.at[k - 1],
            device_id={"mem": lax.rem(me + k, n_mem)},
            device_id_type=MESH,
        )

    for k in range(1, n_mem):
        inc_copy(k).start()

    def x_copy(k):
        return pltpu.make_async_remote_copy(
            src_ref=own.at[k], dst_ref=buf.at[0, k], send_sem=xs.at[k], recv_sem=xr.at[k],
            device_id={"lat": x_peer}, device_id_type=MESH,
        )

    def y_copy(k):
        return pltpu.make_async_remote_copy(
            src_ref=buf.at[0, k], dst_ref=buf.at[1, k], send_sem=ys.at[k], recv_sem=yr.at[k],
            device_id={"lat": y_peer}, device_id_type=MESH,
        )

    def z_copy(k):
        return pltpu.make_async_remote_copy(
            src_ref=buf.at[1, k], dst_ref=buf.at[2, k], send_sem=zs.at[k], recv_sem=zr.at[k],
            device_id={"lat": z_target}, device_id_type=MESH,
        )

    def part_copy(k, c):
        peer = lax.rem(me + k, n_mem)
        return pltpu.make_async_remote_copy(
            src_ref=acc.at[c, :, pl.ds(pl.multiple_of(peer * share, share), share), :],
            dst_ref=part.at[k - 1, c],
            send_sem=ps.at[k - 1, c],
            recv_sem=pr.at[k - 1, c],
            device_id={"mem": peer},
            device_id_type=MESH,
        )

    contract = (((1,), (1,)), ((), ()))
    spot = lax.broadcasted_iota(jnp.int32, (rows, levels), 0)
    level = lax.broadcasted_iota(jnp.int32, (rows, levels), 1)
    expand = jnp.where(lax.div(spot, slab) == level, 1.0, 0.0)
    tall = jnp.dot(expand, vert_ref[...], precision=HIGHEST, preferred_element_type=jnp.float32)
    gram = lax.dot_general(tall, tall, contract, precision=HIGHEST, preferred_element_type=jnp.float32)
    line = lax.rem(lax.broadcasted_iota(jnp.int32, (rows, LANES), 0), slab)
    lane = lax.broadcasted_iota(jnp.int32, (rows, LANES), 1)
    place = lane + (i * slab - reach)
    inside = (place >= 0) & (place < n_lat * slab)

    def band(offset):
        distance = lane - line - offset
        total = jnp.zeros((rows, LANES), jnp.float32)
        for o in range(taps):
            total = jnp.where(distance == o, lat_ref[o], total)
        return total

    left = jnp.where(inside, band(0), 0.0)
    for slot, offset in ((0, slab * 0), (1, slab * (1 - 2 * x)), (2, slab * (2 * x - 1))):
        block = lax.dot_general(
            left, band(offset), contract, precision=HIGHEST, preferred_element_type=jnp.float32
        )
        mats[slot] = gram * block

    @pl.when(corner & jnp.logical_not(z_in))
    def _():
        @pl.loop(0, items)
        def _(k):
            buf[2, k] = jnp.zeros((rows, LANES), jnp.float32)

    lon_count = lon_ref.shape[0]
    lon_taps = [lon_ref[o] for o in range(lon_count)]
    auto = [
        sum(lon_taps[o] * lon_taps[o + d] for o in range(lon_count - d)) for d in range(lon_count)
    ]

    def piece(m, q):
        at = pl.ds(pl.multiple_of(q * PIECE, PIECE), PIECE)
        total = mem_v[m, 0, at, :].astype(jnp.float32) * inc_v[0, at, :]
        for v in range(1, variables):
            total = total + mem_v[m, v, at, :].astype(jnp.float32) * inc_v[v, at, :]
        smooth = auto[0] * total
        for d in range(1, lon_count):
            smooth = smooth + auto[d] * (
                pltpu.roll(total, d, axis=1) + pltpu.roll(total, lon - d, axis=1)
            )
        for c in range(chunks):
            own[m * chunks + c, at, :] = smooth[:, c * LANES : (c + 1) * LANES]

    def send_member(m):
        @pl.loop(0, chunks)
        def _(c):
            x_copy(m * chunks + c).start()

    per_member = rows // PIECE
    per_step = 2 * per_member // chunks

    inc_local.wait()
    for k in range(1, n_mem):
        inc_copy(k).wait_recv()
    for m in range(count):
        load(m).wait()

    @pl.loop(0, per_member)
    def _(q):
        piece(0, q)

    send_member(0)

    far = 1 + jnp.where(corner, 1, 0)

    def post(k):
        m = lax.div(k, chunks)
        c = lax.rem(k, chunks)
        spread = jnp.dot(mats[0], own[k], precision=HIGHEST, preferred_element_type=jnp.float32)
        spread = spread + jnp.dot(
            mats[1], buf[0, k], precision=HIGHEST, preferred_element_type=jnp.float32
        )
        spread = spread + jnp.dot(
            mats[2], buf[far, k], precision=HIGHEST, preferred_element_type=jnp.float32
        )
        across = pl.ds(pl.multiple_of(c * LANES, LANES), LANES)

        @pl.when(m == 0)
        def _():
            for v in range(variables):
                acc[c, v] = mem_v[m, v, :, across].astype(jnp.float32) * spread

        @pl.when(m > 0)
        def _():
            for v in range(variables):
                acc[c, v] += mem_v[m, v, :, across].astype(jnp.float32) * spread

        @pl.when(m == count - 1)
        def _():
            for j in range(1, n_mem):
                part_copy(j, c).start()

    def step(t, carry):
        @pl.when(t < items)
        def _():
            x_copy(t).wait_recv()
            y_copy(t).start()

        @pl.when((t >= 1) & (t < items + 1))
        def _():
            y_copy(t - 1).wait_recv()

            @pl.when(z_out)
            def _():
                z_copy(t - 1).start()

        first = t * per_step + per_member

        @pl.when(first < count * per_member)
        def _():
            m = lax.div(first, per_member)
            q = lax.rem(first, per_member)

            @pl.loop(0, per_step)
            def _(s):
                piece(m, q + s)

            @pl.when(q + per_step == per_member)
            def _():
                send_member(m)

        @pl.when(t >= 2)
        def _():
            @pl.when(z_in)
            def _():
                z_copy(t - 2).wait_recv()

            post(t - 2)

        return carry

    lax.fori_loop(0, items + 2, step, 0)

    scale = jnp.float32(count * n_mem - 1)

    @pl.loop(0, chunks)
    def _(c):
        for j in range(1, n_mem):
            part_copy(j, c).wait_recv()
        across = pl.ds(pl.multiple_of(c * LANES, LANES), LANES)
        for v in range(variables):
            total = acc[c, v, own_rows, :]
            for j in range(1, n_mem):
                total = total + part[j - 1, c, v]
            out_ref[v, :, across] = total / scale

    @pl.loop(0, items)
    def _(k):
        x_copy(k).wait_send()
        y_copy(k).wait_send()

        @pl.when(z_out)
        def _():
            z_copy(k).wait_send()

    for j in range(1, n_mem):
        inc_copy(j).wait_send()

        @pl.loop(0, chunks)
        def _(c):
            part_copy(j, c).wait_send()


def per_device(n_mem, n_lat, members, increment, vertical, lat_taps, lon_taps):
    count, variables, levels, slab, lon = members.shape
    rows = levels * slab
    share = rows // n_mem
    chunks = lon // LANES
    items = count * chunks
    dma = pltpu.SemaphoreType.DMA
    peers = max(n_mem - 1, 1)
    result = pl.pallas_call(
        functools.partial(kernel, n_mem, n_lat, levels),
        out_shape=jax.ShapeDtypeStruct((variables, share, lon), jnp.float32),
        in_specs=[
            pl.BlockSpec(memory_space=pl.ANY),
            pl.BlockSpec(memory_space=pl.ANY),
            pl.BlockSpec(memory_space=pltpu.VMEM),
            pl.BlockSpec(memory_space=pltpu.SMEM),
            pl.BlockSpec(memory_space=pltpu.SMEM),
        ],
        out_specs=pl.BlockSpec(memory_space=pltpu.VMEM),
        scratch_shapes=[
            pltpu.VMEM((count, variables, rows, lon), jnp.bfloat16),
            pltpu.VMEM((variables, rows, lon), jnp.float32),
            pltpu.VMEM((items, rows, LANES), jnp.float32),
            pltpu.VMEM((3, items, rows, LANES), jnp.float32),
            pltpu.VMEM((chunks, variables, rows, LANES), jnp.float32),
            pltpu.VMEM((peers, chunks, variables, share, LANES), jnp.float32),
            pltpu.VMEM((3, rows, rows), jnp.float32),
            dma((count,)),
            dma,
            dma((peers,)),
            dma((peers,)),
            dma((items,)),
            dma((items,)),
            dma((items,)),
            dma((items,)),
            dma((items,)),
            dma((items,)),
            dma((peers, chunks)),
            dma((peers, chunks)),
        ],
        compiler_params=pltpu.CompilerParams(
            collective_id=0, has_side_effects=True, vmem_limit_bytes=44 * 1024 * 1024
        ),
    )(
        members.reshape(count, variables, rows, lon),
        increment.reshape(variables, share, lon),
        vertical,
        lat_taps,
        lon_taps,
    )
    return result.reshape(increment.shape)


def solution(mesh):
    in_specs = (P("mem", None, None, "lat", None), P(None, "mem", "lat", None), P(), P(), P())
    out_specs = P(None, "mem", "lat", None)
    return jax.shard_map(
        functools.partial(per_device, mesh.shape["mem"], mesh.shape["lat"]),
        mesh=mesh, in_specs=in_specs, out_specs=out_specs, check_vma=False,
    )
```

```python
import functools

import jax
import jax.numpy as jnp
from jax import lax
from jax.experimental import pallas as pl
from jax.experimental.pallas import tpu as pltpu
from jax.sharding import PartitionSpec as P

LANES = 128
Y_LAG = 3
Z_LAG = 6
AHEAD = 4
PIECE = 16
HIGHEST = lax.Precision.HIGHEST
MESH = pl.DeviceIdType.MESH


def kernel(
    n_mem, n_lat, levels, members_ref, inc_ref, vert_hbm, lat_hbm, lon_hbm, out_ref,
    vert_ref, lat_ref, lon_ref, small_sem,
    mem_v, inc_v, own, buf, acc, part, mats,
    load_sem, inc_sem, inc_send, inc_recv, xs, xr, ys, yr, zs, zr, ps, pr,
):
    count, variables, rows, lon = mem_v.shape
    slab = rows // levels
    taps = lat_ref.shape[0]
    reach = taps // 2
    chunks = lon // LANES
    items = count * chunks
    share = rows // n_mem
    me = lax.axis_index("mem")
    i = lax.axis_index("lat")
    x = lax.rem(i, 2)
    y = lax.rem(lax.div(i, 2), 2)
    x_peer = i + 1 - 2 * x
    y_peer = i + 2 - 4 * y
    corner = x == y
    z_target = i + 4 - 8 * x
    z_source = i - 4 + 8 * x
    z_out = corner & (z_target >= 0) & (z_target < n_lat)
    z_in = corner & (z_source >= 0) & (z_source < n_lat)

    def load(m):
        return pltpu.make_async_copy(members_ref.at[m], mem_v.at[m], load_sem.at[m])

    own_rows = pl.ds(pl.multiple_of(me * share, share), share)
    inc_local = pltpu.make_async_copy(inc_ref, inc_v.at[:, own_rows, :], inc_sem)
    inc_local.start()
    for m in range(count):
        load(m).start()

    small = [
        pltpu.make_async_copy(source, target, small_sem.at[n])
        for n, (source, target) in enumerate(
            ((vert_hbm, vert_ref), (lat_hbm, lat_ref), (lon_hbm, lon_ref))
        )
    ]
    for copy in small:
        copy.start()

    barrier = pltpu.get_barrier_semaphore()
    for k in range(1, n_mem):
        pl.semaphore_signal(
            barrier, inc=1, device_id={"mem": lax.rem(me + k, n_mem)}, device_id_type=MESH
        )
    pl.semaphore_signal(barrier, inc=1, device_id={"lat": x_peer}, device_id_type=MESH)
    pl.semaphore_signal(barrier, inc=1, device_id={"lat": y_peer}, device_id_type=MESH)

    @pl.when(z_out)
    def _():
        pl.semaphore_signal(barrier, inc=1, device_id={"lat": z_target}, device_id_type=MESH)

    @pl.when(z_in)
    def _():
        pl.semaphore_signal(barrier, inc=1, device_id={"lat": z_source}, device_id_type=MESH)

    pl.semaphore_wait(barrier, n_mem + 1 + z_out.astype(jnp.int32) + z_in.astype(jnp.int32))

    def inc_copy(k):
        return pltpu.make_async_remote_copy(
            src_ref=inc_ref,
            dst_ref=inc_v.at[:, own_rows, :],
            send_sem=inc_send.at[k - 1],
            recv_sem=inc_recv.at[k - 1],
            device_id={"mem": lax.rem(me + k, n_mem)},
            device_id_type=MESH,
        )

    for k in range(1, n_mem):
        inc_copy(k).start()

    def x_copy(k):
        return pltpu.make_async_remote_copy(
            src_ref=own.at[k], dst_ref=buf.at[0, k], send_sem=xs.at[k], recv_sem=xr.at[k],
            device_id={"lat": x_peer}, device_id_type=MESH,
        )

    def y_copy(k):
        return pltpu.make_async_remote_copy(
            src_ref=buf.at[0, k], dst_ref=buf.at[1, k], send_sem=ys.at[k], recv_sem=yr.at[k],
            device_id={"lat": y_peer}, device_id_type=MESH,
        )

    def z_copy(k):
        return pltpu.make_async_remote_copy(
            src_ref=buf.at[1, k], dst_ref=buf.at[2, k], send_sem=zs.at[k], recv_sem=zr.at[k],
            device_id={"lat": z_target}, device_id_type=MESH,
        )

    def part_copy(k, c):
        peer = lax.rem(me + k, n_mem)
        return pltpu.make_async_remote_copy(
            src_ref=acc.at[c, :, pl.ds(pl.multiple_of(peer * share, share), share), :],
            dst_ref=part.at[k - 1, c],
            send_sem=ps.at[k - 1, c],
            recv_sem=pr.at[k - 1, c],
            device_id={"mem": peer},
            device_id_type=MESH,
        )

    for copy in small:
        copy.wait()

    contract = (((1,), (1,)), ((), ()))
    spot = lax.broadcasted_iota(jnp.int32, (rows, levels), 0)
    level = lax.broadcasted_iota(jnp.int32, (rows, levels), 1)
    expand = jnp.where(lax.div(spot, slab) == level, 1.0, 0.0)
    tall = jnp.dot(expand, vert_ref[...], precision=HIGHEST, preferred_element_type=jnp.float32)
    gram = lax.dot_general(tall, tall, contract, precision=HIGHEST, preferred_element_type=jnp.float32)
    line = lax.rem(lax.broadcasted_iota(jnp.int32, (rows, LANES), 0), slab)
    lane = lax.broadcasted_iota(jnp.int32, (rows, LANES), 1)
    place = lane + (i * slab - reach)
    inside = (place >= 0) & (place < n_lat * slab)

    def band(offset):
        distance = lane - line - offset
        total = jnp.zeros((rows, LANES), jnp.float32)
        for o in range(taps):
            total = jnp.where(distance == o, lat_ref[o], total)
        return total

    left = jnp.where(inside, band(0), 0.0)
    for slot, offset in ((0, slab * 0), (1, slab * (1 - 2 * x)), (2, slab * (2 * x - 1))):
        block = lax.dot_general(
            left, band(offset), contract, precision=HIGHEST, preferred_element_type=jnp.float32
        )
        mats[slot] = gram * block

    @pl.when(corner & jnp.logical_not(z_in))
    def _():
        @pl.loop(0, items)
        def _(k):
            buf[2, k] = jnp.zeros((rows, LANES), jnp.float32)

    lon_count = lon_ref.shape[0]
    lon_taps = [lon_ref[o] for o in range(lon_count)]
    auto = [
        sum(lon_taps[o] * lon_taps[o + d] for o in range(lon_count - d)) for d in range(lon_count)
    ]

    def piece(m, q):
        at = pl.ds(pl.multiple_of(q * PIECE, PIECE), PIECE)
        total = mem_v[m, 0, at, :].astype(jnp.float32) * inc_v[0, at, :]
        for v in range(1, variables):
            total = total + mem_v[m, v, at, :].astype(jnp.float32) * inc_v[v, at, :]
        smooth = auto[0] * total
        for d in range(1, lon_count):
            smooth = smooth + auto[d] * (
                pltpu.roll(total, d, axis=1) + pltpu.roll(total, lon - d, axis=1)
            )
        for c in range(chunks):
            own[m * chunks + c, at, :] = smooth[:, c * LANES : (c + 1) * LANES]

    per_member = rows // PIECE
    per_step = 2 * per_member // chunks

    inc_local.wait()
    for k in range(1, n_mem):
        inc_copy(k).wait_recv()
    for m in range(count):
        load(m).wait()

    @pl.loop(0, per_member)
    def _(q):
        piece(0, q)

    @pl.loop(0, AHEAD)
    def _(k):
        x_copy(k).start()

    far = 1 + jnp.where(corner, 1, 0)

    def post(k):
        m = lax.div(k, chunks)
        c = lax.rem(k, chunks)
        spread = jnp.dot(mats[0], own[k], precision=HIGHEST, preferred_element_type=jnp.float32)
        spread = spread + jnp.dot(
            mats[1], buf[0, k], precision=HIGHEST, preferred_element_type=jnp.float32
        )
        spread = spread + jnp.dot(
            mats[2], buf[far, k], precision=HIGHEST, preferred_element_type=jnp.float32
        )
        across = pl.ds(pl.multiple_of(c * LANES, LANES), LANES)

        @pl.when(m == 0)
        def _():
            for v in range(variables):
                acc[c, v] = mem_v[m, v, :, across].astype(jnp.float32) * spread

        @pl.when(m > 0)
        def _():
            for v in range(variables):
                acc[c, v] += mem_v[m, v, :, across].astype(jnp.float32) * spread

        @pl.when(m == count - 1)
        def _():
            for j in range(1, n_mem):
                part_copy(j, c).start()

    def step(t, carry):
        @pl.when(t < items)
        def _():
            x_copy(t).wait_recv()
            y_copy(t).start()

        @pl.when(t + AHEAD < items)
        def _():
            x_copy(t + AHEAD).start()

        @pl.when((t >= Y_LAG) & (t < items + Y_LAG))
        def _():
            y_copy(t - Y_LAG).wait_recv()

            @pl.when(z_out)
            def _():
                z_copy(t - Y_LAG).start()

        first = t * per_step + per_member

        @pl.when(first < count * per_member)
        def _():
            m = lax.div(first, per_member)
            q = lax.rem(first, per_member)

            @pl.loop(0, per_step)
            def _(s):
                piece(m, q + s)

        @pl.when(t >= Z_LAG)
        def _():
            @pl.when(z_in)
            def _():
                z_copy(t - Z_LAG).wait_recv()

            post(t - Z_LAG)

        return carry

    lax.fori_loop(0, items + Z_LAG, step, 0)

    scale = jnp.float32(count * n_mem - 1)

    @pl.loop(0, chunks)
    def _(c):
        for j in range(1, n_mem):
            part_copy(j, c).wait_recv()
        across = pl.ds(pl.multiple_of(c * LANES, LANES), LANES)
        for v in range(variables):
            total = acc[c, v, own_rows, :]
            for j in range(1, n_mem):
                total = total + part[j - 1, c, v]
            out_ref[v, :, across] = total / scale

    @pl.loop(0, items)
    def _(k):
        x_copy(k).wait_send()
        y_copy(k).wait_send()

        @pl.when(z_out)
        def _():
            z_copy(k).wait_send()

    for j in range(1, n_mem):
        inc_copy(j).wait_send()

        @pl.loop(0, chunks)
        def _(c):
            part_copy(j, c).wait_send()


def per_device(n_mem, n_lat, members, increment, vertical, lat_taps, lon_taps):
    count, variables, levels, slab, lon = members.shape
    rows = levels * slab
    share = rows // n_mem
    chunks = lon // LANES
    items = count * chunks
    dma = pltpu.SemaphoreType.DMA
    peers = max(n_mem - 1, 1)
    result = pl.pallas_call(
        functools.partial(kernel, n_mem, n_lat, levels),
        out_shape=jax.ShapeDtypeStruct((variables, share, lon), jnp.float32),
        in_specs=[
            pl.BlockSpec(memory_space=pltpu.HBM),
            pl.BlockSpec(memory_space=pltpu.HBM),
            pl.BlockSpec(memory_space=pltpu.HBM),
            pl.BlockSpec(memory_space=pltpu.HBM),
            pl.BlockSpec(memory_space=pltpu.HBM),
        ],
        out_specs=pl.BlockSpec(memory_space=pltpu.VMEM),
        scratch_shapes=[
            pltpu.VMEM(vertical.shape, jnp.float32),
            pltpu.SMEM(lat_taps.shape, jnp.float32),
            pltpu.SMEM(lon_taps.shape, jnp.float32),
            dma((3,)),
            pltpu.VMEM((count, variables, rows, lon), jnp.bfloat16),
            pltpu.VMEM((variables, rows, lon), jnp.float32),
            pltpu.VMEM((items, rows, LANES), jnp.float32),
            pltpu.VMEM((3, items, rows, LANES), jnp.float32),
            pltpu.VMEM((chunks, variables, rows, LANES), jnp.float32),
            pltpu.VMEM((peers, chunks, variables, share, LANES), jnp.float32),
            pltpu.VMEM((3, rows, rows), jnp.float32),
            dma((count,)),
            dma,
            dma((peers,)),
            dma((peers,)),
            dma((items,)),
            dma((items,)),
            dma((items,)),
            dma((items,)),
            dma((items,)),
            dma((items,)),
            dma((peers, chunks)),
            dma((peers, chunks)),
        ],
        compiler_params=pltpu.CompilerParams(
            collective_id=0, has_side_effects=True, vmem_limit_bytes=60 * 1024 * 1024
        ),
    )(
        members.reshape(count, variables, rows, lon),
        increment.reshape(variables, share, lon),
        vertical,
        lat_taps,
        lon_taps,
    )
    return result.reshape(increment.shape)


def solution(mesh):
    in_specs = (P("mem", None, None, "lat", None), P(None, "mem", "lat", None), P(), P(), P())
    out_specs = P(None, "mem", "lat", None)
    return jax.shard_map(
        functools.partial(per_device, mesh.shape["mem"], mesh.shape["lat"]),
        mesh=mesh, in_specs=in_specs, out_specs=out_specs, check_vma=False,
    )
```

```python
import functools

import jax
import jax.numpy as jnp
from jax import lax
from jax.experimental import pallas as pl
from jax.experimental.pallas import tpu as pltpu
from jax.sharding import PartitionSpec as P

LANES = 128
Y_LAG = 3
Z_LAG = 6
AHEAD = 4
HIGHEST = lax.Precision.HIGHEST
MESH = pl.DeviceIdType.MESH


def kernel(
    n_mem, n_lat, levels, members_ref, inc_ref, vert_hbm, lat_hbm, lon_hbm, out_ref,
    vert_ref, lat_ref, lon_ref, small_sem,
    mem_v, inc_v, own, buf, acc, part, mats,
    load_sem, inc_sem, inc_send, inc_recv, xs, xr, ys, yr, zs, zr, ps, pr,
):
    count, variables, rows, lon = mem_v.shape
    slab = rows // levels
    taps = lat_ref.shape[0]
    reach = taps // 2
    chunks = lon // LANES
    items = count * chunks
    width = rows // chunks
    share = rows // n_mem
    me = lax.axis_index("mem")
    i = lax.axis_index("lat")
    x = lax.rem(i, 2)
    y = lax.rem(lax.div(i, 2), 2)
    x_peer = i + 1 - 2 * x
    y_peer = i + 2 - 4 * y
    corner = x == y
    z_target = i + 4 - 8 * x
    z_source = i - 4 + 8 * x
    z_out = corner & (z_target >= 0) & (z_target < n_lat)
    z_in = corner & (z_source >= 0) & (z_source < n_lat)

    def load(m):
        return pltpu.make_async_copy(members_ref.at[m], mem_v.at[m], load_sem.at[m])

    own_rows = pl.ds(pl.multiple_of(me * share, share), share)
    inc_local = pltpu.make_async_copy(inc_ref, inc_v.at[:, own_rows, :], inc_sem)
    inc_local.start()
    for m in range(count):
        load(m).start()

    small = [
        pltpu.make_async_copy(source, target, small_sem.at[n])
        for n, (source, target) in enumerate(
            ((vert_hbm, vert_ref), (lat_hbm, lat_ref), (lon_hbm, lon_ref))
        )
    ]
    for copy in small:
        copy.start()

    barrier = pltpu.get_barrier_semaphore()
    for k in range(1, n_mem):
        pl.semaphore_signal(
            barrier, inc=1, device_id={"mem": lax.rem(me + k, n_mem)}, device_id_type=MESH
        )
    pl.semaphore_signal(barrier, inc=1, device_id={"lat": x_peer}, device_id_type=MESH)
    pl.semaphore_signal(barrier, inc=1, device_id={"lat": y_peer}, device_id_type=MESH)

    @pl.when(z_out)
    def _():
        pl.semaphore_signal(barrier, inc=1, device_id={"lat": z_target}, device_id_type=MESH)

    @pl.when(z_in)
    def _():
        pl.semaphore_signal(barrier, inc=1, device_id={"lat": z_source}, device_id_type=MESH)

    pl.semaphore_wait(barrier, n_mem + 1 + z_out.astype(jnp.int32) + z_in.astype(jnp.int32))

    def inc_copy(k):
        return pltpu.make_async_remote_copy(
            src_ref=inc_ref,
            dst_ref=inc_v.at[:, own_rows, :],
            send_sem=inc_send.at[k - 1],
            recv_sem=inc_recv.at[k - 1],
            device_id={"mem": lax.rem(me + k, n_mem)},
            device_id_type=MESH,
        )

    for k in range(1, n_mem):
        inc_copy(k).start()

    def own_item(k, early):
        return own.at[:chunks, pl.ds(pl.multiple_of(k * width, width), width), :] if early else own.at[k]

    def item(n, k, early):
        if early:
            return buf.at[n, :chunks, pl.ds(pl.multiple_of(k * width, width), width), :]
        return buf.at[n, k]

    def each(k, act):
        pl.when(k < chunks)(lambda: act(k, True))
        pl.when(k >= chunks)(lambda: act(k, False))

    def x_copy(k, early):
        return pltpu.make_async_remote_copy(
            src_ref=own_item(k, early), dst_ref=item(0, k, early), send_sem=xs.at[k], recv_sem=xr.at[k],
            device_id={"lat": x_peer}, device_id_type=MESH,
        )

    def y_copy(k, early):
        return pltpu.make_async_remote_copy(
            src_ref=item(0, k, early), dst_ref=item(1, k, early), send_sem=ys.at[k], recv_sem=yr.at[k],
            device_id={"lat": y_peer}, device_id_type=MESH,
        )

    def z_copy(k, early):
        return pltpu.make_async_remote_copy(
            src_ref=item(1, k, early), dst_ref=item(2, k, early), send_sem=zs.at[k], recv_sem=zr.at[k],
            device_id={"lat": z_target}, device_id_type=MESH,
        )

    def part_copy(k, c):
        peer = lax.rem(me + k, n_mem)
        return pltpu.make_async_remote_copy(
            src_ref=acc.at[c, :, pl.ds(pl.multiple_of(peer * share, share), share), :],
            dst_ref=part.at[k - 1, c],
            send_sem=ps.at[k - 1, c],
            recv_sem=pr.at[k - 1, c],
            device_id={"mem": peer},
            device_id_type=MESH,
        )

    for copy in small:
        copy.wait()

    contract = (((1,), (1,)), ((), ()))
    spot = lax.broadcasted_iota(jnp.int32, (rows, levels), 0)
    level = lax.broadcasted_iota(jnp.int32, (rows, levels), 1)
    expand = jnp.where(lax.div(spot, slab) == level, 1.0, 0.0)
    tall = jnp.dot(expand, vert_ref[...], precision=HIGHEST, preferred_element_type=jnp.float32)
    gram = lax.dot_general(tall, tall, contract, precision=HIGHEST, preferred_element_type=jnp.float32)
    line = lax.rem(lax.broadcasted_iota(jnp.int32, (rows, LANES), 0), slab)
    lane = lax.broadcasted_iota(jnp.int32, (rows, LANES), 1)
    place = lane + (i * slab - reach)
    inside = (place >= 0) & (place < n_lat * slab)

    def band(offset):
        distance = lane - line - offset
        total = jnp.zeros((rows, LANES), jnp.float32)
        for o in range(taps):
            total = jnp.where(distance == o, lat_ref[o], total)
        return total

    left = jnp.where(inside, band(0), 0.0)
    for slot, offset in ((0, slab * 0), (1, slab * (1 - 2 * x)), (2, slab * (2 * x - 1))):
        block = lax.dot_general(
            left, band(offset), contract, precision=HIGHEST, preferred_element_type=jnp.float32
        )
        mats[slot] = gram * block

    @pl.when(corner & jnp.logical_not(z_in))
    def _():
        @pl.loop(0, items)
        def _(k):
            buf[2, k] = jnp.zeros((rows, LANES), jnp.float32)

    lon_count = lon_ref.shape[0]
    lon_taps = [lon_ref[o] for o in range(lon_count)]
    auto = [
        sum(lon_taps[o] * lon_taps[o + d] for o in range(lon_count - d)) for d in range(lon_count)
    ]

    def piece(m, q):
        at = pl.ds(pl.multiple_of(q * width, width), width)
        total = mem_v[m, 0, at, :].astype(jnp.float32) * inc_v[0, at, :]
        for v in range(1, variables):
            total = total + mem_v[m, v, at, :].astype(jnp.float32) * inc_v[v, at, :]
        smooth = auto[0] * total
        for d in range(1, lon_count):
            smooth = smooth + auto[d] * (
                pltpu.roll(total, d, axis=1) + pltpu.roll(total, lon - d, axis=1)
            )
        for c in range(chunks):
            own[m * chunks + c, at, :] = smooth[:, c * LANES : (c + 1) * LANES]

    per_step = 2

    inc_local.wait()
    for k in range(1, n_mem):
        inc_copy(k).wait_recv()
    load(0).wait()

    @pl.loop(0, chunks)
    def _(q):
        piece(0, q)
        x_copy(q, True).start()

    far = 1 + jnp.where(corner, 1, 0)

    def post(k):
        m = lax.div(k, chunks)
        c = lax.rem(k, chunks)
        spread = jnp.dot(mats[0], own[k], precision=HIGHEST, preferred_element_type=jnp.float32)
        spread = spread + jnp.dot(
            mats[1], buf[0, k], precision=HIGHEST, preferred_element_type=jnp.float32
        )
        spread = spread + jnp.dot(
            mats[2], buf[far, k], precision=HIGHEST, preferred_element_type=jnp.float32
        )
        across = pl.ds(pl.multiple_of(c * LANES, LANES), LANES)

        @pl.when(m == 0)
        def _():
            for v in range(variables):
                acc[c, v] = mem_v[m, v, :, across].astype(jnp.float32) * spread

        @pl.when(m > 0)
        def _():
            for v in range(variables):
                acc[c, v] += mem_v[m, v, :, across].astype(jnp.float32) * spread

        @pl.when(m == count - 1)
        def _():
            for j in range(1, n_mem):
                part_copy(j, c).start()

    def step(t, carry):
        @pl.when(t < items)
        def _():
            def act(k, early):
                x_copy(k, early).wait_recv()
                y_copy(k, early).start()

            each(t, act)

        @pl.when((t + AHEAD >= chunks) & (t + AHEAD < items))
        def _():
            x_copy(t + AHEAD, False).start()

        @pl.when((t >= Y_LAG) & (t < items + Y_LAG))
        def _():
            def act(k, early):
                y_copy(k, early).wait_recv()

                @pl.when(z_out)
                def _():
                    z_copy(k, early).start()

            each(t - Y_LAG, act)

        first = t * per_step + chunks

        @pl.when(first < count * chunks)
        def _():
            m = lax.div(first, chunks)
            q = lax.rem(first, chunks)

            @pl.when(q == 0)
            def _():
                load(m).wait()

            @pl.loop(0, per_step)
            def _(s):
                piece(m, q + s)

        @pl.when(t >= Z_LAG)
        def _():
            @pl.when(z_in)
            def _():
                each(t - Z_LAG, lambda k, early: z_copy(k, early).wait_recv())

        begin = chunks - 1 + Z_LAG

        @pl.when((t >= begin) & (t < begin + chunks - 1))
        def _():
            @pl.loop(0, 2)
            def _(s):
                post(2 * (t - begin) + s)

        @pl.when(t >= begin + chunks - 1)
        def _():
            post(t - Z_LAG)

        return carry

    lax.fori_loop(0, items + Z_LAG, step, 0)

    scale = jnp.float32(count * n_mem - 1)

    @pl.loop(0, chunks)
    def _(c):
        for j in range(1, n_mem):
            part_copy(j, c).wait_recv()
        across = pl.ds(pl.multiple_of(c * LANES, LANES), LANES)
        for v in range(variables):
            total = acc[c, v, own_rows, :]
            for j in range(1, n_mem):
                total = total + part[j - 1, c, v]
            out_ref[v, :, across] = total / scale

    @pl.loop(0, items)
    def _(k):
        def act(k, early):
            x_copy(k, early).wait_send()
            y_copy(k, early).wait_send()

            @pl.when(z_out)
            def _():
                z_copy(k, early).wait_send()

        each(k, act)

    for j in range(1, n_mem):
        inc_copy(j).wait_send()

        @pl.loop(0, chunks)
        def _(c):
            part_copy(j, c).wait_send()


def per_device(n_mem, n_lat, members, increment, vertical, lat_taps, lon_taps):
    count, variables, levels, slab, lon = members.shape
    rows = levels * slab
    share = rows // n_mem
    chunks = lon // LANES
    items = count * chunks
    dma = pltpu.SemaphoreType.DMA
    peers = max(n_mem - 1, 1)
    result = pl.pallas_call(
        functools.partial(kernel, n_mem, n_lat, levels),
        out_shape=jax.ShapeDtypeStruct((variables, share, lon), jnp.float32),
        in_specs=[
            pl.BlockSpec(memory_space=pltpu.HBM),
            pl.BlockSpec(memory_space=pltpu.HBM),
            pl.BlockSpec(memory_space=pltpu.HBM),
            pl.BlockSpec(memory_space=pltpu.HBM),
            pl.BlockSpec(memory_space=pltpu.HBM),
        ],
        out_specs=pl.BlockSpec(memory_space=pltpu.VMEM),
        scratch_shapes=[
            pltpu.VMEM(vertical.shape, jnp.float32),
            pltpu.SMEM(lat_taps.shape, jnp.float32),
            pltpu.SMEM(lon_taps.shape, jnp.float32),
            dma((3,)),
            pltpu.VMEM((count, variables, rows, lon), jnp.bfloat16),
            pltpu.VMEM((variables, rows, lon), jnp.float32),
            pltpu.VMEM((items, rows, LANES), jnp.float32),
            pltpu.VMEM((3, items, rows, LANES), jnp.float32),
            pltpu.VMEM((chunks, variables, rows, LANES), jnp.float32),
            pltpu.VMEM((peers, chunks, variables, share, LANES), jnp.float32),
            pltpu.VMEM((3, rows, rows), jnp.float32),
            dma((count,)),
            dma,
            dma((peers,)),
            dma((peers,)),
            dma((items,)),
            dma((items,)),
            dma((items,)),
            dma((items,)),
            dma((items,)),
            dma((items,)),
            dma((peers, chunks)),
            dma((peers, chunks)),
        ],
        compiler_params=pltpu.CompilerParams(
            collective_id=0, has_side_effects=True, vmem_limit_bytes=60 * 1024 * 1024
        ),
    )(
        members.reshape(count, variables, rows, lon),
        increment.reshape(variables, share, lon),
        vertical,
        lat_taps,
        lon_taps,
    )
    return result.reshape(increment.shape)


def solution(mesh):
    in_specs = (P("mem", None, None, "lat", None), P(None, "mem", "lat", None), P(), P(), P())
    out_specs = P(None, "mem", "lat", None)
    return jax.shard_map(
        functools.partial(per_device, mesh.shape["mem"], mesh.shape["lat"]),
        mesh=mesh, in_specs=in_specs, out_specs=out_specs, check_vma=False,
    )
```

```python
import functools

import jax
import jax.numpy as jnp
from jax import lax
from jax.experimental import pallas as pl
from jax.experimental.pallas import tpu as pltpu
from jax.sharding import PartitionSpec as P

LANES = 128
Y_LAG = 3
Z_LAG = 6
AHEAD = 4
HIGHEST = lax.Precision.HIGHEST
MESH = pl.DeviceIdType.MESH


def kernel(
    n_mem, n_lat, levels, members_ref, inc_ref, vert_hbm, lat_hbm, lon_hbm, out_ref,
    vert_ref, lat_ref, lon_ref, small_sem,
    mem_v, inc_v, own, buf, acc, part, mats,
    load_sem, inc_sem, inc_send, inc_recv, xs, xr, ys, yr, zs, zr, ps, pr,
):
    count, variables, rows, lon = mem_v.shape
    slab = rows // levels
    taps = lat_ref.shape[0]
    reach = taps // 2
    chunks = lon // LANES
    items = count * chunks
    width = rows // chunks
    share = rows // n_mem
    own_bands = share // width if share % width == 0 else 0
    me = lax.axis_index("mem")
    i = lax.axis_index("lat")
    x = lax.rem(i, 2)
    y = lax.rem(lax.div(i, 2), 2)
    x_peer = i + 1 - 2 * x
    y_peer = i + 2 - 4 * y
    corner = x == y
    z_target = i + 4 - 8 * x
    z_source = i - 4 + 8 * x
    z_out = corner & (z_target >= 0) & (z_target < n_lat)
    z_in = corner & (z_source >= 0) & (z_source < n_lat)

    def load(m):
        return pltpu.make_async_copy(members_ref.at[m], mem_v.at[m], load_sem.at[m])

    own_rows = pl.ds(pl.multiple_of(me * share, share), share)
    inc_local = pltpu.make_async_copy(inc_ref, inc_v.at[:, own_rows, :], inc_sem)
    inc_local.start()
    for m in range(count):
        load(m).start()

    small = [
        pltpu.make_async_copy(source, target, small_sem.at[n])
        for n, (source, target) in enumerate(
            ((vert_hbm, vert_ref), (lat_hbm, lat_ref), (lon_hbm, lon_ref))
        )
    ]
    for copy in small:
        copy.start()

    barrier = pltpu.get_barrier_semaphore()
    for k in range(1, n_mem):
        pl.semaphore_signal(
            barrier, inc=1, device_id={"mem": lax.rem(me + k, n_mem)}, device_id_type=MESH
        )
    pl.semaphore_signal(barrier, inc=1, device_id={"lat": x_peer}, device_id_type=MESH)
    pl.semaphore_signal(barrier, inc=1, device_id={"lat": y_peer}, device_id_type=MESH)

    @pl.when(z_out)
    def _():
        pl.semaphore_signal(barrier, inc=1, device_id={"lat": z_target}, device_id_type=MESH)

    @pl.when(z_in)
    def _():
        pl.semaphore_signal(barrier, inc=1, device_id={"lat": z_source}, device_id_type=MESH)

    pl.semaphore_wait(barrier, n_mem + 1 + z_out.astype(jnp.int32) + z_in.astype(jnp.int32))

    def inc_copy(k):
        return pltpu.make_async_remote_copy(
            src_ref=inc_ref,
            dst_ref=inc_v.at[:, own_rows, :],
            send_sem=inc_send.at[k - 1],
            recv_sem=inc_recv.at[k - 1],
            device_id={"mem": lax.rem(me + k, n_mem)},
            device_id_type=MESH,
        )

    for k in range(1, n_mem):
        inc_copy(k).start()

    def band_rows(k):
        turn = lax.rem(me * own_bands + k, chunks)
        return pl.ds(pl.multiple_of(turn * width, width), width)

    def own_item(k, early):
        return own.at[:chunks, band_rows(k), :] if early else own.at[k]

    def item(n, k, early):
        if early:
            return buf.at[n, :chunks, band_rows(k), :]
        return buf.at[n, k]

    def each(k, act):
        pl.when(k < chunks)(lambda: act(k, True))
        pl.when(k >= chunks)(lambda: act(k, False))

    def x_copy(k, early):
        return pltpu.make_async_remote_copy(
            src_ref=own_item(k, early), dst_ref=item(0, k, early), send_sem=xs.at[k], recv_sem=xr.at[k],
            device_id={"lat": x_peer}, device_id_type=MESH,
        )

    def y_copy(k, early):
        return pltpu.make_async_remote_copy(
            src_ref=item(0, k, early), dst_ref=item(1, k, early), send_sem=ys.at[k], recv_sem=yr.at[k],
            device_id={"lat": y_peer}, device_id_type=MESH,
        )

    def z_copy(k, early):
        return pltpu.make_async_remote_copy(
            src_ref=item(1, k, early), dst_ref=item(2, k, early), send_sem=zs.at[k], recv_sem=zr.at[k],
            device_id={"lat": z_target}, device_id_type=MESH,
        )

    def part_copy(k, c):
        peer = lax.rem(me + k, n_mem)
        return pltpu.make_async_remote_copy(
            src_ref=acc.at[c, :, pl.ds(pl.multiple_of(peer * share, share), share), :],
            dst_ref=part.at[k - 1, c],
            send_sem=ps.at[k - 1, c],
            recv_sem=pr.at[k - 1, c],
            device_id={"mem": peer},
            device_id_type=MESH,
        )

    for copy in small:
        copy.wait()

    lon_count = lon_ref.shape[0]
    lon_taps = [lon_ref[o] for o in range(lon_count)]
    auto = [
        sum(lon_taps[o] * lon_taps[o + d] for o in range(lon_count - d)) for d in range(lon_count)
    ]

    def piece(m, q):
        at = pl.ds(pl.multiple_of(q * width, width), width)
        total = mem_v[m, 0, at, :].astype(jnp.float32) * inc_v[0, at, :]
        for v in range(1, variables):
            total = total + mem_v[m, v, at, :].astype(jnp.float32) * inc_v[v, at, :]
        smooth = auto[0] * total
        for d in range(1, lon_count):
            smooth = smooth + auto[d] * (
                pltpu.roll(total, d, axis=1) + pltpu.roll(total, lon - d, axis=1)
            )
        for c in range(chunks):
            own[m * chunks + c, at, :] = smooth[:, c * LANES : (c + 1) * LANES]

    per_step = 2

    def first_band(k):
        piece(0, lax.rem(me * own_bands + k, chunks))
        x_copy(k, True).start()

    inc_local.wait()
    load(0).wait()
    pl.loop(0, own_bands)(first_band)

    contract = (((1,), (1,)), ((), ()))
    spot = lax.broadcasted_iota(jnp.int32, (rows, levels), 0)
    level = lax.broadcasted_iota(jnp.int32, (rows, levels), 1)
    expand = jnp.where(lax.div(spot, slab) == level, 1.0, 0.0)
    tall = jnp.dot(expand, vert_ref[...], precision=HIGHEST, preferred_element_type=jnp.float32)
    gram = lax.dot_general(tall, tall, contract, precision=HIGHEST, preferred_element_type=jnp.float32)
    line = lax.rem(lax.broadcasted_iota(jnp.int32, (rows, LANES), 0), slab)
    lane = lax.broadcasted_iota(jnp.int32, (rows, LANES), 1)
    place = lane + (i * slab - reach)
    inside = (place >= 0) & (place < n_lat * slab)

    def band(offset):
        distance = lane - line - offset
        total = jnp.zeros((rows, LANES), jnp.float32)
        for o in range(taps):
            total = jnp.where(distance == o, lat_ref[o], total)
        return total

    left = jnp.where(inside, band(0), 0.0)
    for slot, offset in ((0, slab * 0), (1, slab * (1 - 2 * x)), (2, slab * (2 * x - 1))):
        block = lax.dot_general(
            left, band(offset), contract, precision=HIGHEST, preferred_element_type=jnp.float32
        )
        mats[slot] = gram * block

    @pl.when(corner & jnp.logical_not(z_in))
    def _():
        @pl.loop(0, items)
        def _(k):
            buf[2, k] = jnp.zeros((rows, LANES), jnp.float32)

    for k in range(1, n_mem):
        inc_copy(k).wait_recv()
    pl.loop(own_bands, chunks)(first_band)

    far = 1 + jnp.where(corner, 1, 0)

    def post(k):
        m = lax.div(k, chunks)
        c = lax.rem(k, chunks)
        spread = jnp.dot(mats[0], own[k], precision=HIGHEST, preferred_element_type=jnp.float32)
        spread = spread + jnp.dot(
            mats[1], buf[0, k], precision=HIGHEST, preferred_element_type=jnp.float32
        )
        spread = spread + jnp.dot(
            mats[2], buf[far, k], precision=HIGHEST, preferred_element_type=jnp.float32
        )
        across = pl.ds(pl.multiple_of(c * LANES, LANES), LANES)

        @pl.when(m == 0)
        def _():
            for v in range(variables):
                acc[c, v] = mem_v[m, v, :, across].astype(jnp.float32) * spread

        @pl.when(m > 0)
        def _():
            for v in range(variables):
                acc[c, v] += mem_v[m, v, :, across].astype(jnp.float32) * spread

        @pl.when(m == count - 1)
        def _():
            for j in range(1, n_mem):
                part_copy(j, c).start()

    def step(t, carry):
        @pl.when(t < items)
        def _():
            def act(k, early):
                x_copy(k, early).wait_recv()
                y_copy(k, early).start()

            each(t, act)

        @pl.when((t + AHEAD >= chunks) & (t + AHEAD < items))
        def _():
            x_copy(t + AHEAD, False).start()

        @pl.when((t >= Y_LAG) & (t < items + Y_LAG))
        def _():
            def act(k, early):
                y_copy(k, early).wait_recv()

                @pl.when(z_out)
                def _():
                    z_copy(k, early).start()

            each(t - Y_LAG, act)

        first = t * per_step + chunks

        @pl.when(first < count * chunks)
        def _():
            m = lax.div(first, chunks)
            q = lax.rem(first, chunks)

            @pl.when(q == 0)
            def _():
                load(m).wait()

            @pl.loop(0, per_step)
            def _(s):
                piece(m, q + s)

        @pl.when(t >= Z_LAG)
        def _():
            @pl.when(z_in)
            def _():
                each(t - Z_LAG, lambda k, early: z_copy(k, early).wait_recv())

        begin = chunks - 1 + Z_LAG

        @pl.when((t >= begin) & (t < begin + chunks - 1))
        def _():
            @pl.loop(0, 2)
            def _(s):
                post(2 * (t - begin) + s)

        @pl.when(t >= begin + chunks - 1)
        def _():
            post(t - Z_LAG)

        return carry

    lax.fori_loop(0, items + Z_LAG, step, 0)

    scale = jnp.float32(count * n_mem - 1)

    @pl.loop(0, chunks)
    def _(c):
        for j in range(1, n_mem):
            part_copy(j, c).wait_recv()
        across = pl.ds(pl.multiple_of(c * LANES, LANES), LANES)
        for v in range(variables):
            total = acc[c, v, own_rows, :]
            for j in range(1, n_mem):
                total = total + part[j - 1, c, v]
            out_ref[v, :, across] = total / scale

    @pl.loop(0, items)
    def _(k):
        def act(k, early):
            x_copy(k, early).wait_send()
            y_copy(k, early).wait_send()

            @pl.when(z_out)
            def _():
                z_copy(k, early).wait_send()

        each(k, act)

    for j in range(1, n_mem):
        inc_copy(j).wait_send()

        @pl.loop(0, chunks)
        def _(c):
            part_copy(j, c).wait_send()


def per_device(n_mem, n_lat, members, increment, vertical, lat_taps, lon_taps):
    count, variables, levels, slab, lon = members.shape
    rows = levels * slab
    share = rows // n_mem
    chunks = lon // LANES
    items = count * chunks
    dma = pltpu.SemaphoreType.DMA
    peers = max(n_mem - 1, 1)
    result = pl.pallas_call(
        functools.partial(kernel, n_mem, n_lat, levels),
        out_shape=jax.ShapeDtypeStruct((variables, share, lon), jnp.float32),
        in_specs=[
            pl.BlockSpec(memory_space=pltpu.HBM),
            pl.BlockSpec(memory_space=pltpu.HBM),
            pl.BlockSpec(memory_space=pltpu.HBM),
            pl.BlockSpec(memory_space=pltpu.HBM),
            pl.BlockSpec(memory_space=pltpu.HBM),
        ],
        out_specs=pl.BlockSpec(memory_space=pltpu.VMEM),
        scratch_shapes=[
            pltpu.VMEM(vertical.shape, jnp.float32),
            pltpu.SMEM(lat_taps.shape, jnp.float32),
            pltpu.SMEM(lon_taps.shape, jnp.float32),
            dma((3,)),
            pltpu.VMEM((count, variables, rows, lon), jnp.bfloat16),
            pltpu.VMEM((variables, rows, lon), jnp.float32),
            pltpu.VMEM((items, rows, LANES), jnp.float32),
            pltpu.VMEM((3, items, rows, LANES), jnp.float32),
            pltpu.VMEM((chunks, variables, rows, LANES), jnp.float32),
            pltpu.VMEM((peers, chunks, variables, share, LANES), jnp.float32),
            pltpu.VMEM((3, rows, rows), jnp.float32),
            dma((count,)),
            dma,
            dma((peers,)),
            dma((peers,)),
            dma((items,)),
            dma((items,)),
            dma((items,)),
            dma((items,)),
            dma((items,)),
            dma((items,)),
            dma((peers, chunks)),
            dma((peers, chunks)),
        ],
        compiler_params=pltpu.CompilerParams(
            collective_id=0, has_side_effects=True, vmem_limit_bytes=60 * 1024 * 1024
        ),
    )(
        members.reshape(count, variables, rows, lon),
        increment.reshape(variables, share, lon),
        vertical,
        lat_taps,
        lon_taps,
    )
    return result.reshape(increment.shape)


def solution(mesh):
    in_specs = (P("mem", None, None, "lat", None), P(None, "mem", "lat", None), P(), P(), P())
    out_specs = P(None, "mem", "lat", None)
    return jax.shard_map(
        functools.partial(per_device, mesh.shape["mem"], mesh.shape["lat"]),
        mesh=mesh, in_specs=in_specs, out_specs=out_specs, check_vma=False,
    )
```

```python
import functools

import jax
import jax.numpy as jnp
from jax import lax
from jax.experimental import pallas as pl
from jax.experimental.pallas import tpu as pltpu
from jax.sharding import PartitionSpec as P

LANES = 128
Y_LAG = 3
Z_LAG = 6
AHEAD = 4
HIGHEST = lax.Precision.HIGHEST
MESH = pl.DeviceIdType.MESH


def kernel(
    n_mem, n_lat, levels, members_ref, inc_ref, vert_hbm, lat_hbm, lon_hbm, out_ref,
    vert_ref, lat_ref, lon_ref, small_sem,
    mem_v, inc_v, own, buf, acc, part, mats,
    load_sem, inc_sem, inc_send, inc_recv, xs, xr, ys, yr, zs, zr, ps, pr,
):
    count, variables, rows, lon = mem_v.shape
    slab = rows // levels
    taps = lat_ref.shape[0]
    reach = taps // 2
    chunks = lon // LANES
    items = count * chunks
    width = rows // chunks
    share = rows // n_mem
    own_bands = share // width if share % width == 0 else 0
    me = lax.axis_index("mem")
    i = lax.axis_index("lat")
    x = lax.rem(i, 2)
    y = lax.rem(lax.div(i, 2), 2)
    x_peer = i + 1 - 2 * x
    y_peer = i + 2 - 4 * y
    corner = x == y
    z_target = i + 4 - 8 * x
    z_source = i - 4 + 8 * x
    z_out = corner & (z_target >= 0) & (z_target < n_lat)
    z_in = corner & (z_source >= 0) & (z_source < n_lat)

    def load(m):
        return pltpu.make_async_copy(members_ref.at[m], mem_v.at[m], load_sem.at[m])

    own_rows = pl.ds(pl.multiple_of(me * share, share), share)
    inc_local = pltpu.make_async_copy(inc_ref, inc_v.at[:, own_rows, :], inc_sem)
    inc_local.start()
    for m in range(count):
        load(m).start()

    small = [
        pltpu.make_async_copy(source, target, small_sem.at[n])
        for n, (source, target) in enumerate(
            ((vert_hbm, vert_ref), (lat_hbm, lat_ref), (lon_hbm, lon_ref))
        )
    ]
    for copy in small:
        copy.start()

    barrier = pltpu.get_barrier_semaphore()
    for k in range(1, n_mem):
        pl.semaphore_signal(
            barrier, inc=1, device_id={"mem": lax.rem(me + k, n_mem)}, device_id_type=MESH
        )
    pl.semaphore_signal(barrier, inc=1, device_id={"lat": x_peer}, device_id_type=MESH)
    pl.semaphore_signal(barrier, inc=1, device_id={"lat": y_peer}, device_id_type=MESH)

    @pl.when(z_out)
    def _():
        pl.semaphore_signal(barrier, inc=1, device_id={"lat": z_target}, device_id_type=MESH)

    @pl.when(z_in)
    def _():
        pl.semaphore_signal(barrier, inc=1, device_id={"lat": z_source}, device_id_type=MESH)

    pl.semaphore_wait(barrier, n_mem + 1 + z_out.astype(jnp.int32) + z_in.astype(jnp.int32))

    def inc_copy(k):
        return pltpu.make_async_remote_copy(
            src_ref=inc_ref,
            dst_ref=inc_v.at[:, own_rows, :],
            send_sem=inc_send.at[k - 1],
            recv_sem=inc_recv.at[k - 1],
            device_id={"mem": lax.rem(me + k, n_mem)},
            device_id_type=MESH,
        )

    for k in range(1, n_mem):
        inc_copy(k).start()

    def band_rows(k):
        turn = lax.rem(me * own_bands + k, chunks)
        return pl.ds(pl.multiple_of(turn * width, width), width)

    def own_item(k, early):
        return own.at[:chunks, band_rows(k), :] if early else own.at[k]

    def item(n, k, early):
        if early:
            return buf.at[n, :chunks, band_rows(k), :]
        return buf.at[n, k]

    def each(k, act):
        pl.when(k < chunks)(lambda: act(k, True))
        pl.when(k >= chunks)(lambda: act(k, False))

    def x_copy(k, early):
        return pltpu.make_async_remote_copy(
            src_ref=own_item(k, early), dst_ref=item(0, k, early), send_sem=xs.at[k], recv_sem=xr.at[k],
            device_id={"lat": x_peer}, device_id_type=MESH,
        )

    def y_copy(k, early):
        return pltpu.make_async_remote_copy(
            src_ref=item(0, k, early), dst_ref=item(1, k, early), send_sem=ys.at[k], recv_sem=yr.at[k],
            device_id={"lat": y_peer}, device_id_type=MESH,
        )

    def z_copy(k, early):
        return pltpu.make_async_remote_copy(
            src_ref=item(1, k, early), dst_ref=item(2, k, early), send_sem=zs.at[k], recv_sem=zr.at[k],
            device_id={"lat": z_target}, device_id_type=MESH,
        )

    def part_copy(k, c):
        peer = lax.rem(me + k, n_mem)
        return pltpu.make_async_remote_copy(
            src_ref=acc.at[c, :, pl.ds(pl.multiple_of(peer * share, share), share), :],
            dst_ref=part.at[k - 1, c],
            send_sem=ps.at[k - 1, c],
            recv_sem=pr.at[k - 1, c],
            device_id={"mem": peer},
            device_id_type=MESH,
        )

    for copy in small:
        copy.wait()

    lon_count = lon_ref.shape[0]
    lon_taps = [lon_ref[o] for o in range(lon_count)]
    auto = [
        sum(lon_taps[o] * lon_taps[o + d] for o in range(lon_count - d)) for d in range(lon_count)
    ]

    def piece(m, q):
        at = pl.ds(pl.multiple_of(q * width, width), width)
        total = mem_v[m, 0, at, :].astype(jnp.float32) * inc_v[0, at, :]
        for v in range(1, variables):
            total = total + mem_v[m, v, at, :].astype(jnp.float32) * inc_v[v, at, :]
        smooth = auto[0] * total
        for d in range(1, lon_count):
            smooth = smooth + auto[d] * (
                pltpu.roll(total, d, axis=1) + pltpu.roll(total, lon - d, axis=1)
            )
        for c in range(chunks):
            own[m * chunks + c, at, :] = smooth[:, c * LANES : (c + 1) * LANES]

    per_step = 2

    def first_band(k):
        piece(0, lax.rem(me * own_bands + k, chunks))
        x_copy(k, True).start()

    inc_local.wait()
    load(0).wait()
    pl.loop(0, own_bands)(first_band)

    contract = (((1,), (1,)), ((), ()))
    spot = lax.broadcasted_iota(jnp.int32, (rows, levels), 0)
    level = lax.broadcasted_iota(jnp.int32, (rows, levels), 1)
    expand = jnp.where(lax.div(spot, slab) == level, 1.0, 0.0)
    tall = jnp.dot(expand, vert_ref[...], precision=HIGHEST, preferred_element_type=jnp.float32)
    gram = lax.dot_general(tall, tall, contract, precision=HIGHEST, preferred_element_type=jnp.float32)
    line = lax.rem(lax.broadcasted_iota(jnp.int32, (rows, LANES), 0), slab)
    lane = lax.broadcasted_iota(jnp.int32, (rows, LANES), 1)
    place = lane + (i * slab - reach)
    inside = (place >= 0) & (place < n_lat * slab)

    def band(offset):
        distance = lane - line - offset
        total = jnp.zeros((rows, LANES), jnp.float32)
        for o in range(taps):
            total = jnp.where(distance == o, lat_ref[o], total)
        return total

    left = jnp.where(inside, band(0), 0.0)
    for slot, offset in ((0, slab * 0), (1, slab * (1 - 2 * x)), (2, slab * (2 * x - 1))):
        block = lax.dot_general(
            left, band(offset), contract, precision=HIGHEST, preferred_element_type=jnp.float32
        )
        mats[slot] = gram * block

    @pl.when(corner & jnp.logical_not(z_in))
    def _():
        @pl.loop(0, items)
        def _(k):
            buf[2, k] = jnp.zeros((rows, LANES), jnp.float32)

    for k in range(1, n_mem):
        inc_copy(k).wait_recv()
    pl.loop(own_bands, chunks)(first_band)

    far = 1 + jnp.where(corner, 1, 0)

    def post(k):
        m = lax.div(k, chunks)
        c = lax.rem(k, chunks)
        spread = jnp.dot(mats[0], own[k], precision=HIGHEST, preferred_element_type=jnp.float32)
        spread = spread + jnp.dot(
            mats[1], buf[0, k], precision=HIGHEST, preferred_element_type=jnp.float32
        )
        spread = spread + jnp.dot(
            mats[2], buf[far, k], precision=HIGHEST, preferred_element_type=jnp.float32
        )
        across = pl.ds(pl.multiple_of(c * LANES, LANES), LANES)

        @pl.when(m == 0)
        def _():
            for v in range(variables):
                acc[c, v] = mem_v[m, v, :, across].astype(jnp.float32) * spread

        @pl.when(m > 0)
        def _():
            for v in range(variables):
                acc[c, v] += mem_v[m, v, :, across].astype(jnp.float32) * spread

        @pl.when(m == count - 1)
        def _():
            for j in range(1, n_mem):
                part_copy(j, c).start()

    def step(t, carry):
        @pl.when(t < items)
        def _():
            def act(k, early):
                x_copy(k, early).wait_recv()
                y_copy(k, early).start()

            each(t, act)

        @pl.when((t + AHEAD >= chunks) & (t + AHEAD < items))
        def _():
            x_copy(t + AHEAD, False).start()

        @pl.when((t >= Y_LAG) & (t < items + Y_LAG))
        def _():
            def act(k, early):
                y_copy(k, early).wait_recv()

                @pl.when(z_out)
                def _():
                    z_copy(k, early).start()

            each(t - Y_LAG, act)

        first = t * per_step + chunks

        @pl.when(first < count * chunks)
        def _():
            m = lax.div(first, chunks)
            q = lax.rem(first, chunks)

            @pl.when(q == 0)
            def _():
                load(m).wait()

            @pl.loop(0, per_step)
            def _(s):
                piece(m, q + s)

        @pl.when(t >= Z_LAG)
        def _():
            @pl.when(z_in)
            def _():
                each(t - Z_LAG, lambda k, early: z_copy(k, early).wait_recv())

        begin = chunks - 1 + Z_LAG

        @pl.when((t >= begin) & (t < begin + chunks - 1))
        def _():
            @pl.loop(0, 2)
            def _(s):
                post(2 * (t - begin) + s)

        @pl.when(t >= begin + chunks - 1)
        def _():
            post(t - Z_LAG)

        return carry

    lax.fori_loop(0, items + Z_LAG, step, 0)

    @pl.loop(0, items)
    def _(k):
        def act(k, early):
            x_copy(k, early).wait_send()
            y_copy(k, early).wait_send()

            @pl.when(z_out)
            def _():
                z_copy(k, early).wait_send()

        each(k, act)

    scale = jnp.float32(count * n_mem - 1)

    @pl.loop(0, chunks)
    def _(c):
        for j in range(1, n_mem):
            part_copy(j, c).wait_recv()
        across = pl.ds(pl.multiple_of(c * LANES, LANES), LANES)
        for v in range(variables):
            total = acc[c, v, own_rows, :]
            for j in range(1, n_mem):
                total = total + part[j - 1, c, v]
            out_ref[v, :, across] = total / scale

    for j in range(1, n_mem):
        inc_copy(j).wait_send()

        @pl.loop(0, chunks)
        def _(c):
            part_copy(j, c).wait_send()


def per_device(n_mem, n_lat, members, increment, vertical, lat_taps, lon_taps):
    count, variables, levels, slab, lon = members.shape
    rows = levels * slab
    share = rows // n_mem
    chunks = lon // LANES
    items = count * chunks
    dma = pltpu.SemaphoreType.DMA
    peers = max(n_mem - 1, 1)
    result = pl.pallas_call(
        functools.partial(kernel, n_mem, n_lat, levels),
        out_shape=jax.ShapeDtypeStruct((variables, share, lon), jnp.float32),
        in_specs=[
            pl.BlockSpec(memory_space=pltpu.HBM),
            pl.BlockSpec(memory_space=pltpu.HBM),
            pl.BlockSpec(memory_space=pltpu.HBM),
            pl.BlockSpec(memory_space=pltpu.HBM),
            pl.BlockSpec(memory_space=pltpu.HBM),
        ],
        out_specs=pl.BlockSpec(memory_space=pltpu.VMEM),
        scratch_shapes=[
            pltpu.VMEM(vertical.shape, jnp.float32),
            pltpu.SMEM(lat_taps.shape, jnp.float32),
            pltpu.SMEM(lon_taps.shape, jnp.float32),
            dma((3,)),
            pltpu.VMEM((count, variables, rows, lon), jnp.bfloat16),
            pltpu.VMEM((variables, rows, lon), jnp.float32),
            pltpu.VMEM((items, rows, LANES), jnp.float32),
            pltpu.VMEM((3, items, rows, LANES), jnp.float32),
            pltpu.VMEM((chunks, variables, rows, LANES), jnp.float32),
            pltpu.VMEM((peers, chunks, variables, share, LANES), jnp.float32),
            pltpu.VMEM((3, rows, rows), jnp.float32),
            dma((count,)),
            dma,
            dma((peers,)),
            dma((peers,)),
            dma((items,)),
            dma((items,)),
            dma((items,)),
            dma((items,)),
            dma((items,)),
            dma((items,)),
            dma((peers, chunks)),
            dma((peers, chunks)),
        ],
        compiler_params=pltpu.CompilerParams(
            collective_id=0, has_side_effects=True, vmem_limit_bytes=60 * 1024 * 1024
        ),
    )(
        members.reshape(count, variables, rows, lon),
        increment.reshape(variables, share, lon),
        vertical,
        lat_taps,
        lon_taps,
    )
    return result.reshape(increment.shape)


def solution(mesh):
    in_specs = (P("mem", None, None, "lat", None), P(None, "mem", "lat", None), P(), P(), P())
    out_specs = P(None, "mem", "lat", None)
    return jax.shard_map(
        functools.partial(per_device, mesh.shape["mem"], mesh.shape["lat"]),
        mesh=mesh, in_specs=in_specs, out_specs=out_specs, check_vma=False,
    )
```
